128 devices in a mesh: dp: 8 (over x, core), tensor: 16 (over y, z).
Axes of the slice: x: 4, y: 4, z: 4, core: 2. Of those that a mesh axis runs over, the one named last changes fastest.
Arguments:
- tokens: bfloat16 [2048, 4096], P('dp', 'tensor'), may hold values from -6 to 6
- grad_out: bfloat16 [2048, 4096], P('dp', 'tensor'), may hold values from -6 to 6
- w_gate: bfloat16 [4096, 14336], P(None, 'tensor'), may hold values from -0.09375 to 0.09375
- w_up: bfloat16 [4096, 14336], P(None, 'tensor'), may hold values from -0.09375 to 0.09375
- w_down: bfloat16 [14336, 4096], P('tensor'), may hold values from -0.046875 to 0.046875
- active_ids: int32 [8, 56], P('dp'), may hold values from 0 to 111, as said below
- active_count: int32 [8], P('dp'), may hold values from 14 to 56
Outputs:
- input_grad: bfloat16 [2048, 4096], P('dp', 'tensor')
- grad_gate: bfloat16 [4096, 14336], P('dp', 'tensor')
- grad_up: bfloat16 [4096, 14336], P('dp', 'tensor')
- grad_down: bfloat16 [14336, 4096], P('tensor', 'dp')
The draws below stay inside these ranges and needn't reach their ends.
Inputs may be any that keep to these rules, and one draw needn't show every extreme that they name: `active_ids`: each row lists 56 distinct block numbers; only the first active_count entries of a row are active.
All inputs are finite; a program needn't handle non-finite values.
Results may differ from the reference program's by a relative error of at most 0.019.
Values may be sent and summed in bfloat16 or wider, within the bound.
No kernel may reach another device: no remote copies, remote signals or barrier semaphores. Data moves between devices by JAX's collectives and lax.ppermute only.
A program may use at most 192 MiB of HBM per device.

```python
import jax
import jax.numpy as jnp
from jax import lax

D = 4096
BLOCK = 128
NBLK = 112
TILE = 256
MAXACT = 56
TOK_DEV = 256
FF = 14336
TOKENS = 2048
TILES = 8
N_DP = 8


def draw_active_ids(key, part):
    key = jax.random.fold_in(key, 11)
    hot_key, noise_key = jax.random.split(key)
    hotness = jax.random.randint(hot_key, (NBLK,), 0, 4)
    noise = jax.random.randint(noise_key, (TILES, NBLK), 0, 65536)
    scores = (hotness[None, :] * 65536 + noise) * NBLK + jnp.arange(NBLK)[None, :]
    order = jnp.argsort(-scores, axis=1)
    return order[:, :MAXACT].astype(jnp.int32)


def draw_active_count(key, part):
    key = jax.random.fold_in(key, 23)
    counts = jax.random.randint(key, (TILES,), MAXACT // 4, MAXACT + 1)
    counts = counts.at[0].set(MAXACT).at[1].set(MAXACT // 4)
    return counts.astype(jnp.int32)


def block_scale(own_key, dims, cuts, smallest, high):
    gain = 1.0
    for axis_at, shards_of in cuts:
        draws = jax.random.uniform(jax.random.fold_in(jax.random.fold_in(own_key, 6), axis_at), (shards_of,), jnp.float32, smallest / len(cuts), high / len(cuts))
        gain = gain * jnp.repeat(jnp.exp(draws), dims[axis_at] // shards_of).reshape((-1,) + (1,) * (len(dims) - 1 - axis_at))
    return gain


def centred(own_key, dims, width, bound, cuts=(), kind=jnp.bfloat16):
    gain = block_scale(own_key, dims, cuts, -0.22, 0.18) if cuts else 1.0
    array = jax.random.normal(own_key, dims, jnp.float32) * width * gain
    return jnp.minimum(jnp.maximum(array, -bound), bound).astype(kind)


def setup_inputs(seed: int = 0) -> dict:
    key_list = jax.random.split(jax.random.key(seed), 8)
    return {
        "tokens": centred(key_list[0], (TOKENS, D), 1.0, 6.0, ((0, 8), (1, 16))),
        "grad_out": centred(key_list[1], (TOKENS, D), 1.0, 6.0, ((0, 8), (1, 16))),
        "w_gate": centred(key_list[2], (D, FF), D ** -0.5, 0.09375, ((1, 16),)),
        "w_up": centred(key_list[3], (D, FF), D ** -0.5, 0.09375, ((1, 16),)),
        "w_down": centred(key_list[4], (FF, D), FF ** -0.5, 0.046875, ((0, 16),)),
        "active_ids": draw_active_ids(jax.random.fold_in(key_list[7], 71), 0),
        "active_count": draw_active_count(jax.random.fold_in(key_list[7], 71), 0),
    }


def reference(tokens, grad_out, w_gate, w_up, w_down, active_ids, active_count):
    blocks = jnp.arange(NBLK, dtype=jnp.int32)
    in_range = jnp.arange(MAXACT, dtype=jnp.int32)[None, :] < active_count[:, None]
    matches = (active_ids[:, :, None] == blocks[None, None, :]) & in_range[:, :, None]
    tile_mask = jnp.any(matches, axis=1).astype(jnp.float32)
    row_mask = jnp.broadcast_to(tile_mask[:, None, :, None], (TILES, TILE, NBLK, BLOCK)).reshape(TOKENS, FF)
    gate = jnp.dot(tokens, w_gate, preferred_element_type=jnp.float32)
    up = jnp.dot(tokens, w_up, preferred_element_type=jnp.float32)
    logistic = jax.nn.sigmoid(gate)
    swish = gate * logistic
    hidden = (swish * up * row_mask).astype(jnp.bfloat16)
    hidden_grad = lax.dot_general(grad_out, w_down, (((1,), (1,)), ((), ())), preferred_element_type=jnp.float32)
    d_gate = (hidden_grad * up * logistic * (1.0 + gate * (1.0 - logistic)) * row_mask).astype(jnp.bfloat16)
    d_up = (hidden_grad * swish * row_mask).astype(jnp.bfloat16)
    input_grad = lax.dot_general(d_gate, w_gate, (((1,), (1,)), ((), ())), preferred_element_type=jnp.float32)
    input_grad = input_grad + lax.dot_general(d_up, w_up, (((1,), (1,)), ((), ())), preferred_element_type=jnp.float32)
    input_grad = input_grad.astype(jnp.bfloat16)
    members = (tokens.reshape(N_DP, TOK_DEV, D), grad_out.reshape(N_DP, TOK_DEV, D),
               d_gate.reshape(N_DP, TOK_DEV, FF), d_up.reshape(N_DP, TOK_DEV, FF), hidden.reshape(N_DP, TOK_DEV, FF))

    def add_group(totals, member):
        tok_part, cot_part, gate_part, up_part, hid_part = member
        partials = (jnp.dot(tok_part.T, gate_part, preferred_element_type=jnp.float32).astype(jnp.bfloat16),
                    jnp.dot(tok_part.T, up_part, preferred_element_type=jnp.float32).astype(jnp.bfloat16),
                    jnp.dot(hid_part.T, cot_part, preferred_element_type=jnp.float32).astype(jnp.bfloat16))
        partials = lax.optimization_barrier(partials)
        return tuple(t + p.astype(jnp.float32) for t, p in zip(totals, partials)), None

    start_totals = (jnp.zeros((D, FF), jnp.float32), jnp.zeros((D, FF), jnp.float32), jnp.zeros((FF, D), jnp.float32))
    totals, _ = lax.scan(add_group, start_totals, members)
    return (input_grad, totals[0].astype(jnp.bfloat16), totals[1].astype(jnp.bfloat16), totals[2].astype(jnp.bfloat16))
```

```python
import jax
import jax.numpy as jnp
from jax import lax
from jax.experimental import pallas as pl
from jax.experimental.pallas import tpu as pltpu
from jax.sharding import Mesh, PartitionSpec as P

BLOCK = 128
RING = 4
OFFSETS = (0, 1, 3, 2)


def from_offset(value, axis, offset):
    return lax.ppermute(value, axis, [(i, (i - offset) % RING) for i in range(RING)])


def gather_ring(stack, axis):
    half = stack.shape[1] // 2
    after = from_offset(stack, axis, 1)
    before = from_offset(stack, axis, 3)
    low = from_offset(after[:, :half], axis, 1)
    high = from_offset(before[:, half:], axis, 3)
    return jnp.concatenate([stack, after, before, jnp.concatenate([low, high], axis=1)], axis=0)


def forward_kernel(jt, jg, active, x, dy, wg, wu, wd, out, gate_acc, up_acc, hid_acc):
    step = pl.program_id(0)
    nblk = out.shape[1] // 3 // BLOCK
    f_local = nblk * BLOCK
    gate_part = jnp.dot(x[0], wg[...], preferred_element_type=jnp.float32)
    up_part = jnp.dot(x[0], wu[...], preferred_element_type=jnp.float32)
    hid_part = lax.dot_general(
        dy[0], wd[...], (((1,), (1,)), ((), ())), preferred_element_type=jnp.float32
    )

    @pl.when(step == 0)
    def _():
        gate_acc[...] = gate_part
        up_acc[...] = up_part
        hid_acc[...] = hid_part

    @pl.when(step > 0)
    def _():
        gate_acc[...] += gate_part
        up_acc[...] += up_part
        hid_acc[...] += hid_part

    @pl.when(step == pl.num_programs(0) - 1)
    def _():
        for b in range(nblk):
            cols = pl.ds(b * BLOCK, BLOCK)
            on = active[b] > 0
            gate, up, hid = gate_acc[:, cols], up_acc[:, cols], hid_acc[:, cols]
            logistic = jax.nn.sigmoid(gate)
            swish = gate * logistic
            hidden = swish * up
            d_gate = hid * up * logistic * (1.0 + gate * (1.0 - logistic))
            d_up = hid * swish
            for k, value in enumerate((hidden, d_gate, d_up)):
                out[:, pl.ds(k * f_local + b * BLOCK, BLOCK)] = jnp.where(on, value, 0.0).astype(
                    out.dtype
                )


def forward(jt, jg, active, x, dy, wg, wu, wd):
    n, rows, depth = x.shape
    f_local = wg.shape[1]
    return pl.pallas_call(
        forward_kernel,
        grid_spec=pltpu.PrefetchScalarGridSpec(
            num_scalar_prefetch=3,
            grid=(n,),
            in_specs=[
                pl.BlockSpec((1, rows, depth), lambda i, jt, jg, a: (i, 0, 0)),
                pl.BlockSpec((1, rows, depth), lambda i, jt, jg, a: (i, 0, 0)),
                pl.BlockSpec((depth, f_local), lambda i, jt, jg, a: (jt[i], 0)),
                pl.BlockSpec((depth, f_local), lambda i, jt, jg, a: (jt[i], 0)),
                pl.BlockSpec((f_local, depth), lambda i, jt, jg, a: (0, jg[i])),
            ],
            out_specs=pl.BlockSpec((rows, 3 * f_local), lambda i, jt, jg, a: (0, 0)),
            scratch_shapes=[pltpu.VMEM((rows, f_local), jnp.float32)] * 3,
        ),
        out_shape=jax.ShapeDtypeStruct((rows, 3 * f_local), jnp.bfloat16),
        compiler_params=pltpu.CompilerParams(vmem_limit_bytes=40 * 2**20),
        cost_estimate=pl.CostEstimate(
            flops=6 * n * rows * depth * f_local,
            bytes_accessed=6 * n * depth * f_local + 4 * n * rows * depth,
            transcendentals=rows * f_local,
        ),
        name="forward",
    )(jt, jg, active, x, dy, wg, wu, wd)


def backward_kernel(js, act, wg, wu, out):
    f_local = wg.shape[1]
    rows_t = (((1,), (1,)), ((), ()))
    total = lax.dot_general(
        act[:, pl.ds(f_local, f_local)], wg[...], rows_t, preferred_element_type=jnp.float32
    )
    total += lax.dot_general(
        act[:, pl.ds(2 * f_local, f_local)], wu[...], rows_t, preferred_element_type=jnp.float32
    )
    out[0] = total.astype(out.dtype)


def backward(js, act, wg, wu):
    n = js.shape[0]
    rows = act.shape[0]
    d_model, f_local = wg.shape
    depth = d_model // n
    return pl.pallas_call(
        backward_kernel,
        grid_spec=pltpu.PrefetchScalarGridSpec(
            num_scalar_prefetch=1,
            grid=(n,),
            in_specs=[
                pl.BlockSpec((rows, 3 * f_local), lambda i, js: (0, 0)),
                pl.BlockSpec((depth, f_local), lambda i, js: (js[i], 0)),
                pl.BlockSpec((depth, f_local), lambda i, js: (js[i], 0)),
            ],
            out_specs=pl.BlockSpec((1, rows, depth), lambda i, js: (i, 0, 0)),
        ),
        out_shape=jax.ShapeDtypeStruct((n, rows, depth), jnp.bfloat16),
        compiler_params=pltpu.CompilerParams(vmem_limit_bytes=40 * 2**20),
        cost_estimate=pl.CostEstimate(
            flops=4 * rows * d_model * f_local,
            bytes_accessed=4 * d_model * f_local + 2 * rows * d_model,
            transcendentals=0,
        ),
        name="backward",
    )(js, act, wg, wu)


def weights_kernel(index, *refs):
    acts, pieces = refs[:10], refs[10]
    out_gate, out_up, out_down = refs[11:14]
    act_buf, piece_buf, gate_acc, up_acc, down_acc, act_sem, piece_sem = refs[14:]
    tiles, rows, wide = act_buf.shape
    f_local = wide // 3
    depth = piece_buf.shape[2]
    half = rows // 2
    copies = []
    for t in range(tiles):
        mine = []
        if t % 4 == 3:
            parts = [(acts[t // 4 * 5 + 3], 0, half), (acts[t // 4 * 5 + 4], half, half)]
        else:
            parts = [(acts[t // 4 * 5 + t % 4], 0, rows)]
        for p, (ref, start, size) in enumerate(parts):
            mine.append(
                pltpu.make_async_copy(ref, act_buf.at[t, pl.ds(start, size)], act_sem.at[t, p])
            )
        for h in range(2):
            mine.append(
                pltpu.make_async_copy(
                    pieces.at[index[t, h]], piece_buf.at[2 * t + h], piece_sem.at[t, h]
                )
            )
        copies.append(mine)
    for mine in copies:
        for copy in mine:
            copy.start()
    first_t = (((0,), (0,)), ((), ()))
    for t in range(tiles):
        for copy in copies[t]:
            copy.wait()
        for h in range(2):
            tok = piece_buf[2 * t + h, pl.ds(0, rows), :]
            cot = piece_buf[2 * t + h, pl.ds(rows, rows), :]
            cols = pl.ds(h * depth, depth)
            g = lax.dot_general(
                tok, act_buf[t, :, pl.ds(f_local, f_local)], first_t,
                preferred_element_type=jnp.float32,
            )
            u = lax.dot_general(
                tok, act_buf[t, :, pl.ds(2 * f_local, f_local)], first_t,
                preferred_element_type=jnp.float32,
            )
            d = lax.dot_general(
                act_buf[t, :, pl.ds(0, f_local)], cot, first_t,
                preferred_element_type=jnp.float32,
            )
            if t == 0:
                gate_acc[cols, :] = g
                up_acc[cols, :] = u
                down_acc[:, cols] = d
            elif t < tiles - 1:
                gate_acc[cols, :] += g
                up_acc[cols, :] += u
                down_acc[:, cols] += d
            else:
                out_gate[cols, :] = (gate_acc[cols, :] + g).astype(out_gate.dtype)
                out_up[cols, :] = (up_acc[cols, :] + u).astype(out_up.dtype)
                out_down[:, cols] = (down_acc[:, cols] + d).astype(out_down.dtype)


def weight_grads(index, acts, pieces):
    tiles = index.shape[0]
    rows, wide = acts[0].shape
    f_local = wide // 3
    depth = pieces.shape[2]
    anywhere = pl.BlockSpec(memory_space=pl.ANY)
    whole = pl.BlockSpec(memory_space=pltpu.VMEM)
    return pl.pallas_call(
        weights_kernel,
        in_specs=[pl.BlockSpec(memory_space=pltpu.SMEM)] + [anywhere] * 11,
        out_specs=[whole] * 3,
        out_shape=[
            jax.ShapeDtypeStruct((2 * depth, f_local), jnp.bfloat16),
            jax.ShapeDtypeStruct((2 * depth, f_local), jnp.bfloat16),
            jax.ShapeDtypeStruct((f_local, 2 * depth), jnp.bfloat16),
        ],
        scratch_shapes=[
            pltpu.VMEM((tiles, rows, wide), jnp.bfloat16),
            pltpu.VMEM((2 * tiles, 2 * rows, depth), jnp.bfloat16),
            pltpu.VMEM((2 * depth, f_local), jnp.float32),
            pltpu.VMEM((2 * depth, f_local), jnp.float32),
            pltpu.VMEM((f_local, 2 * depth), jnp.float32),
            pltpu.SemaphoreType.DMA((tiles, 2)),
            pltpu.SemaphoreType.DMA((tiles, 2)),
        ],
        compiler_params=pltpu.CompilerParams(vmem_limit_bytes=48 * 2**20),
        cost_estimate=pl.CostEstimate(
            flops=2 * tiles * rows * 2 * depth * wide,
            bytes_accessed=2 * tiles * rows * wide + 4 * tiles * rows * 2 * depth,
            transcendentals=0,
        ),
        name="weight_grads",
    )(index, *acts, pieces)


def per_device(tokens, grad_out, w_gate, w_up, w_down, active_ids, active_count):
    rows, depth = tokens.shape
    f_local = w_gate.shape[1]
    nblk = f_local // BLOCK
    x, c, y, z = (lax.axis_index(a) for a in ("x", "c", "y", "z"))
    off = jnp.array(OFFSETS, jnp.int32)

    to_columns = [
        (
            ((sx * 2 + sc) * 4 + sy) * 4 + sz,
            ((sy * 2 + sz // 2) * 4 + sx) * 4 + (sz % 2) * 2 + sc,
        )
        for sx in range(4)
        for sc in range(2)
        for sy in range(4)
        for sz in range(4)
    ]
    both = jnp.concatenate([tokens, grad_out], axis=0)
    turned = lax.ppermute(both, ("x", "c", "y", "z"), to_columns)
    pieces = lax.all_gather(turned, ("y", "z"))

    x_rel = gather_ring(gather_ring(tokens[None], "z"), "y")
    dy_rel = gather_ring(gather_ring(grad_out[None], "y"), "z")
    slow, fast = jnp.repeat(off, 4), jnp.tile(off, 4)
    jt = (y + slow) % 4 * 4 + (z + fast) % 4
    jg = (y + fast) % 4 * 4 + (z + slow) % 4

    block_ids = (y * 4 + z) * nblk + jnp.arange(nblk, dtype=jnp.int32)
    listed = jnp.arange(active_ids.shape[1], dtype=jnp.int32) < active_count[0]
    matches = (active_ids[0][:, None] == block_ids[None, :]) & listed[:, None]
    active = jnp.any(matches, axis=0).astype(jnp.int32)

    act = forward(jt, jg, active, x_rel, dy_rel, w_gate, w_up, w_down)

    half = rows // 2
    after = from_offset(act, "x", 1)
    before = from_offset(act, "x", 3)
    low = from_offset(after[:half], "x", 1)
    high = from_offset(before[half:], "x", 3)
    acts = [act, after, before, low, high]
    swapped = [lax.ppermute(a, "c", [(0, 1), (1, 0)]) for a in acts]

    partial_dx = backward(jnp.arange(16, dtype=jnp.int32), act, w_gate, w_up)
    shares = lax.all_to_all(partial_dx, ("y", "z"), 0, 0)
    input_grad = jnp.sum(shares.astype(jnp.float32), axis=0).astype(jnp.bfloat16)

    tile_x = (x + off) % 4
    index = jnp.concatenate(
        [
            tile_x[:, None] * 4 + jnp.array([0, 2], jnp.int32)[None, :] + core
            for core in (c, 1 - c)
        ]
    )
    grads = weight_grads(index.astype(jnp.int32), acts + swapped, pieces)
    return (input_grad, *grads)


def solution(mesh):
    fine = Mesh(mesh.devices.reshape(4, 2, 4, 4), ("x", "c", "y", "z"))
    dp, tensor = ("x", "c"), ("y", "z")
    in_specs = (
        P(dp, tensor),
        P(dp, tensor),
        P(None, tensor),
        P(None, tensor),
        P(tensor, None),
        P(dp, None),
        P(dp),
    )
    out_specs = (P(dp, tensor), P(dp, tensor), P(dp, tensor), P(tensor, dp))
    return jax.shard_map(
        per_device, mesh=fine, in_specs=in_specs, out_specs=out_specs, check_vma=False
    )
```

```python
import jax
import jax.numpy as jnp
from jax import lax
from jax.experimental import pallas as pl
from jax.experimental.pallas import tpu as pltpu
from jax.sharding import Mesh, PartitionSpec as P

BLOCK = 128
RING = 4
OFFSETS = (0, 1, 3, 2)
MIB = 2**20

IN_VMEM = pl.BlockSpec(memory_space=pltpu.VMEM)
IN_SMEM = pl.BlockSpec(memory_space=pltpu.SMEM)
ANYWHERE = pl.BlockSpec(memory_space=pl.ANY)


def from_offset(value, axis, offset):
    return lax.ppermute(value, axis, [(i, (i - offset) % RING) for i in range(RING)])


def place_of(offset):
    offset = lax.rem(offset + RING, RING)
    return jnp.where(offset < 2, offset, 5 - offset)


def nn(a, b):
    return jnp.dot(a, b, preferred_element_type=jnp.float32)


def nt(a, b):
    return lax.dot_general(a, b, (((1,), (1,)), ((), ())), preferred_element_type=jnp.float32)


def tn(a, b):
    return lax.dot_general(a, b, (((0,), (0,)), ((), ())), preferred_element_type=jnp.float32)


def relay(value, *behind):
    def kernel(*refs):
        refs[-1][...] = refs[0][...]

    return pl.pallas_call(
        kernel,
        in_specs=[IN_VMEM] + [ANYWHERE] * len(behind),
        out_specs=IN_VMEM,
        out_shape=jax.ShapeDtypeStruct(value.shape, value.dtype),
        compiler_params=pltpu.CompilerParams(vmem_limit_bytes=4 * MIB),
        cost_estimate=pl.CostEstimate(
            flops=0, bytes_accessed=4 * value.size, transcendentals=0
        ),
        name="relay",
    )(value, *behind)


def halves(after, before, behind):
    rows, cols = after.shape
    half = rows // 2

    def kernel(after, before, behind, low, high, sems):
        copies = [
            pltpu.make_async_copy(after.at[pl.ds(0, half)], low, sems.at[0]),
            pltpu.make_async_copy(before.at[pl.ds(half, half)], high, sems.at[1]),
        ]
        for copy in copies:
            copy.start()
        for copy in copies:
            copy.wait()

    return pl.pallas_call(
        kernel,
        in_specs=[ANYWHERE] * 3,
        out_specs=[IN_VMEM] * 2,
        out_shape=[jax.ShapeDtypeStruct((half, cols), after.dtype)] * 2,
        scratch_shapes=[pltpu.SemaphoreType.DMA((2,))],
        compiler_params=pltpu.CompilerParams(vmem_limit_bytes=4 * MIB),
        cost_estimate=pl.CostEstimate(
            flops=0, bytes_accessed=4 * rows * cols, transcendentals=0
        ),
        name="halves",
    )(after, before, behind)


def group_buffers(depth, f_local, count):
    return [
        pltpu.VMEM((count, 4 * depth, f_local), jnp.bfloat16),
        pltpu.VMEM((count, 4 * depth, f_local), jnp.bfloat16),
        pltpu.VMEM((count, f_local, 4 * depth), jnp.bfloat16),
        pltpu.SemaphoreType.DMA((6 * count,)),
    ]


def fetch_group(coords, s, offset, weights, buffers):
    wg, wu, wd = weights
    wg_buf, wu_buf, wd_buf, sems = buffers
    wide = wg_buf.shape[1]
    depth = wide // 4
    row, col = lax.rem(coords[2] + offset, 4), lax.rem(coords[3] + offset, 4)
    rows = pl.ds(pl.multiple_of(row * wide, wide), wide)
    views = [(wg.at[rows], wg_buf.at[s]), (wu.at[rows], wu_buf.at[s])]
    for k in range(4):
        cols = pl.ds(pl.multiple_of((4 * k + col) * depth, depth), depth)
        views.append((wd.at[:, cols], wd_buf.at[s, :, pl.ds(k * depth, depth)]))
    copies = [
        pltpu.make_async_copy(source, target, sems.at[6 * s + j])
        for j, (source, target) in enumerate(views)
    ]
    for copy in copies:
        copy.start()
    return copies


def group_terms(coords, s, x, dy, copies, buffers):
    y, z = coords[2], coords[3]
    x = jnp.concatenate([x[place_of(k - z)] for k in range(4)], axis=1)
    copies[0].wait()
    yield nn(x, buffers[0][s])
    copies[1].wait()
    yield nn(x, buffers[1][s])
    dy = jnp.concatenate([dy[place_of(k - y)] for k in range(4)], axis=1)
    for copy in copies[2:]:
        copy.wait()
    yield nt(dy, buffers[2][s])


def forward_first(coords, x, dy, weights):
    rows, depth = x.shape[1:]
    f_local = weights[0].shape[1]

    def kernel(coords, x, dy, wg, wu, wd, *refs):
        outs, held, sems, buffers = refs[:3], refs[3], refs[4], refs[5:]
        loads = [
            pltpu.make_async_copy(piece, held.at[k], sems.at[k]) for k, piece in enumerate((x, dy))
        ]
        for load in loads:
            load.start()
        copies = fetch_group(coords, 0, 0, (wg, wu, wd), buffers)
        for load in loads:
            load.wait()
        for out, term in zip(outs, group_terms(coords, 0, held.at[0], held.at[1], copies, buffers)):
            out[...] = term

    return pl.pallas_call(
        kernel,
        in_specs=[IN_SMEM] + [ANYWHERE] * 5,
        out_specs=[IN_VMEM] * 3,
        out_shape=[jax.ShapeDtypeStruct((rows, f_local), jnp.float32)] * 3,
        scratch_shapes=[
            pltpu.VMEM((2, 4, rows, depth), jnp.bfloat16),
            pltpu.SemaphoreType.DMA((2,)),
        ]
        + group_buffers(depth, f_local, 1),
        compiler_params=pltpu.CompilerParams(vmem_limit_bytes=48 * MIB),
        cost_estimate=pl.CostEstimate(
            flops=24 * rows * depth * f_local,
            bytes_accessed=24 * depth * f_local,
            transcendentals=0,
        ),
        name="forward_first",
    )(coords, x, dy, *weights)


def forward_more(coords, offsets, xs, dys, weights, sums, active):
    count = len(offsets)
    rows, depth = xs[0].shape[1:]
    f_local = weights[0].shape[1]
    nblk = f_local // BLOCK
    last = active is not None

    def kernel(coords, *refs):
        on, refs = (refs[0], refs[1:]) if last else (None, refs)
        pieces, weights = refs[: 2 * count], refs[2 * count : 2 * count + 3]
        olds, refs = refs[2 * count + 3 : 2 * count + 6], refs[2 * count + 6 :]
        outs, refs = (refs[:1], refs[1:]) if last else (refs[:3], refs[3:])
        accs, old_bufs, held, sems, buffers = refs[:3], refs[3:6], refs[6], refs[7], refs[8:]
        groups = []
        for s, offset in enumerate(offsets):
            loads = [
                pltpu.make_async_copy(pieces[k], held.at[k], sems.at[k]) for k in (s, count + s)
            ]
            for load in loads:
                load.start()
            groups.append((loads, fetch_group(coords, s, offset, weights, buffers)))
        old_loads = [
            pltpu.make_async_copy(old, old_buf, sems.at[2 * count + k])
            for k, (old, old_buf) in enumerate(zip(olds, old_bufs))
        ]
        for load in old_loads:
            load.start()
        for s, (loads, copies) in enumerate(groups):
            for load in loads:
                load.wait()
            terms = group_terms(coords, s, held.at[s], held.at[count + s], copies, buffers)
            for acc, term in zip(accs, terms):
                acc[...] = term if s == 0 else acc[...] + term
        for load in old_loads:
            load.wait()
        if not last:
            for out, acc, old in zip(outs, accs, old_bufs):
                out[...] = acc[...] + old[...]
            return
        for b in range(nblk):
            cols = pl.ds(b * BLOCK, BLOCK)
            gate, up, hid = (acc[:, cols] + old[:, cols] for acc, old in zip(accs, old_bufs))
            logistic = jax.nn.sigmoid(gate)
            swish = gate * logistic
            values = (
                swish * up,
                hid * up * logistic * (1.0 + gate * (1.0 - logistic)),
                hid * swish,
            )
            for k, value in enumerate(values):
                outs[0][:, pl.ds(k * f_local + b * BLOCK, BLOCK)] = jnp.where(
                    on[b] > 0, value, 0.0
                ).astype(outs[0].dtype)

    act_shape = jax.ShapeDtypeStruct((rows, 3 * f_local), jnp.bfloat16)
    sum_shape = jax.ShapeDtypeStruct((rows, f_local), jnp.float32)
    return pl.pallas_call(
        kernel,
        in_specs=[IN_SMEM] * (2 if last else 1) + [ANYWHERE] * (2 * count + 6),
        out_specs=IN_VMEM if last else [IN_VMEM] * 3,
        out_shape=act_shape if last else [sum_shape] * 3,
        scratch_shapes=[pltpu.VMEM((rows, f_local), jnp.float32)] * 6
        + [
            pltpu.VMEM((2 * count, 4, rows, depth), jnp.bfloat16),
            pltpu.SemaphoreType.DMA((2 * count + 3,)),
        ]
        + group_buffers(depth, f_local, count),
        compiler_params=pltpu.CompilerParams(vmem_limit_bytes=48 * MIB),
        cost_estimate=pl.CostEstimate(
            flops=24 * count * rows * depth * f_local,
            bytes_accessed=24 * count * depth * f_local,
            transcendentals=rows * f_local if last else 0,
        ),
        name="forward_last" if last else "forward_near",
    )(coords, *([active] if last else []), *xs, *dys, *weights, *sums)


def backward(act, wg, wu):
    rows = act.shape[0]
    d_model, f_local = wg.shape
    n = 16
    depth = d_model // n
    wide = 4 * depth

    def kernel(act, wg, wu, out, wg_buf, wu_buf, sems):
        copies = []
        for i in range(4):
            at = pl.ds(i * wide, wide)
            copies.append(
                (
                    pltpu.make_async_copy(wg.at[at], wg_buf.at[at], sems.at[2 * i]),
                    pltpu.make_async_copy(wu.at[at], wu_buf.at[at], sems.at[2 * i + 1]),
                )
            )
        for pair in copies:
            for copy in pair:
                copy.start()
        d_gate, d_up = (act[:, pl.ds(k * f_local, f_local)] for k in (1, 2))
        for i, pair in enumerate(copies):
            at = pl.ds(i * wide, wide)
            for copy in pair:
                copy.wait()
            total = (nt(d_gate, wg_buf[at]) + nt(d_up, wu_buf[at])).astype(out.dtype)
            for k in range(4):
                out[4 * i + k] = total[:, k * depth : (k + 1) * depth]

    return pl.pallas_call(
        kernel,
        in_specs=[IN_VMEM] + [ANYWHERE] * 2,
        out_specs=IN_VMEM,
        out_shape=jax.ShapeDtypeStruct((n, rows, depth), jnp.bfloat16),
        scratch_shapes=[
            pltpu.VMEM(wg.shape, jnp.bfloat16),
            pltpu.VMEM(wu.shape, jnp.bfloat16),
            pltpu.SemaphoreType.DMA((8,)),
        ],
        compiler_params=pltpu.CompilerParams(vmem_limit_bytes=50 * MIB),
        cost_estimate=pl.CostEstimate(
            flops=4 * rows * d_model * f_local,
            bytes_accessed=4 * d_model * f_local,
            transcendentals=0,
        ),
        name="backward",
    )(act, wg, wu)


def weight_grads(coords, tiles, pieces):
    count, chunk = len(tiles), 4
    parts = [part for _, _, tile in tiles for part in tile]
    wide = parts[0].shape[1]
    rows = pieces.shape[1] // 2
    f_local = wide // 3
    depth = pieces.shape[2]
    cols = 2 * depth
    shapes = [(cols, f_local), (cols, f_local), (f_local, cols)]

    def kernel(coords, *refs):
        acts, refs = list(refs[: len(parts)]), refs[len(parts) :]
        pieces, outs, mark, accs, results = refs[0], refs[1:4], refs[4], refs[5:8], refs[8:11]
        act_buf, tok_buf, cot_buf, sems = refs[11:]
        mark[...] = jnp.zeros_like(mark)
        x, c = coords[0], coords[1]
        used = [0]

        def start(source, target):
            copy = pltpu.make_async_copy(source, target, sems.at[used[0]])
            used[0] += 1
            copy.start()
            return copy

        loads = []
        for t, (offset, other, tile) in enumerate(tiles):
            mine, at = [], t * rows
            for part in tile:
                mine.append(start(acts.pop(0), act_buf.at[pl.ds(at, part.shape[0])]))
                at += part.shape[0]
            core = 1 - c if other else c
            for h in range(2):
                piece = lax.rem(x + offset, RING) * RING + core + 2 * h
                for k, buf in enumerate((tok_buf, cot_buf)):
                    target = buf.at[pl.ds(t * rows, rows), pl.ds(h * depth, depth)]
                    mine.append(start(pieces.at[piece, pl.ds(k * rows, rows)], target))
            loads.append(mine)
        stores = []
        for t in range(0, count, chunk):
            for load in sum(loads[t : t + chunk], []):
                load.wait()
            at = pl.ds(t * rows, chunk * rows)
            for k in range(3):
                if k < 2:
                    term = tn(tok_buf[at], act_buf[at, pl.ds((k + 1) * f_local, f_local)])
                else:
                    term = tn(act_buf[at, pl.ds(0, f_local)], cot_buf[at])
                if t > 0:
                    term = accs[k][...] + term
                if t + chunk < count:
                    accs[k][...] = term
                else:
                    results[k][...] = term.astype(results[k].dtype)
                    stores.append(start(results[k], outs[k]))
        for store in stores:
            store.wait()

    return pl.pallas_call(
        kernel,
        in_specs=[IN_SMEM] + [ANYWHERE] * (len(parts) + 1),
        out_specs=[ANYWHERE] * 3 + [IN_VMEM],
        out_shape=[jax.ShapeDtypeStruct(shape, jnp.bfloat16) for shape in shapes + [(16, 128)]],
        scratch_shapes=[pltpu.VMEM(shape, jnp.float32) for shape in shapes]
        + [pltpu.VMEM(shape, jnp.bfloat16) for shape in shapes]
        + [
            pltpu.VMEM((count * rows, wide), jnp.bfloat16),
            pltpu.VMEM((count * rows, cols), jnp.bfloat16),
            pltpu.VMEM((count * rows, cols), jnp.bfloat16),
            pltpu.SemaphoreType.DMA((len(parts) + 4 * count + 3,)),
        ],
        compiler_params=pltpu.CompilerParams(vmem_limit_bytes=58 * MIB),
        cost_estimate=pl.CostEstimate(
            flops=4 * count * rows * depth * wide,
            bytes_accessed=2 * count * rows * (wide + 4 * depth),
            transcendentals=0,
        ),
        name="weight_grads",
    )(coords, *parts, pieces)


def sum_shares(shares, behind):
    n, rows, cols = shares.shape

    def kernel(shares, behind, out):
        total = shares[0].astype(jnp.float32)
        for k in range(1, n):
            total += shares[k].astype(jnp.float32)
        out[...] = total.astype(out.dtype)

    return pl.pallas_call(
        kernel,
        in_specs=[IN_VMEM, ANYWHERE],
        out_specs=IN_VMEM,
        out_shape=jax.ShapeDtypeStruct((rows, cols), shares.dtype),
        compiler_params=pltpu.CompilerParams(vmem_limit_bytes=8 * MIB),
        cost_estimate=pl.CostEstimate(
            flops=n * rows * cols, bytes_accessed=2 * n * rows * cols, transcendentals=0
        ),
        name="sum_shares",
    )(shares, behind)


def to_columns():
    order = [(x, c, y, z) for x in range(4) for c in range(2) for y in range(4) for z in range(4)]
    flat = lambda x, c, y, z: ((x * 2 + c) * 4 + y) * 4 + z
    return [(flat(x, c, y, z), flat(y, z // 2, x, z % 2 * 2 + c)) for x, c, y, z in order]


def per_device(tokens, grad_out, w_gate, w_up, w_down, active_ids, active_count):
    rows, depth = tokens.shape
    half = rows // 2
    f_local = w_gate.shape[1]
    nblk = f_local // BLOCK
    x, c, y, z = (lax.axis_index(a) for a in ("x", "c", "y", "z"))
    coords = jnp.stack([x, c, y, z]).astype(jnp.int32)

    tok, cot = tokens[None], grad_out[None]
    tok_near = [from_offset(tok, "z", o) for o in OFFSETS[1:]]
    cot_near = [from_offset(cot, "y", o) for o in OFFSETS[1:]]
    tok_row = jnp.concatenate([tok] + tok_near, axis=0)
    cot_row = jnp.concatenate([cot] + cot_near, axis=0)
    tok_after, tok_before = from_offset(tok_row, "y", 1), from_offset(tok_row, "y", 3)
    cot_after, cot_before = from_offset(cot_row, "z", 1), from_offset(cot_row, "z", 3)
    tok_low = from_offset(tok_after[:, :half], "y", 1)
    tok_high = from_offset(tok_before[:, half:], "y", 3)
    cot_low = from_offset(cot_after[:, :half], "z", 1)
    cot_high = from_offset(cot_before[:, half:], "z", 3)
    tok_far = jnp.concatenate([tok_low, tok_high], axis=1)
    cot_far = jnp.concatenate([cot_low, cot_high], axis=1)

    block_ids = (y * 4 + z) * nblk + jnp.arange(nblk, dtype=jnp.int32)
    listed = jnp.arange(active_ids.shape[1], dtype=jnp.int32) < active_count[0]
    matches = (active_ids[0][:, None] == block_ids[None, :]) & listed[:, None]
    active = jnp.any(matches, axis=0).astype(jnp.int32)

    weights = (w_gate, w_up, w_down)
    sums = forward_first(coords, tok_row, cot_row, weights)
    sums = forward_more(
        coords, [1, 3], [tok_after, tok_before], [cot_after, cot_before], weights, sums, None
    )
    both = jnp.concatenate([tokens, grad_out], axis=0)
    both = relay(both, tok_after, cot_after)
    turned = lax.ppermute(both, ("x", "c", "y", "z"), to_columns())
    pieces = lax.all_gather(relay(turned, tok_far, cot_far, sums[0]), ("y", "z"))

    act = forward_more(coords, [2], [tok_far], [cot_far], weights, sums, active)

    after, before = from_offset(act, "x", 1), from_offset(act, "x", 3)
    partial_dx = backward(act, w_gate, w_up)
    shares = lax.all_to_all(partial_dx, ("y", "z"), 0, 0)
    low, high = halves(after, before, partial_dx)
    far = [from_offset(low, "x", 1), from_offset(high, "x", 3)]
    swap = lambda a: lax.ppermute(a, "c", [(0, 1), (1, 0)])
    tiles = [(0, False, [act]), (1, False, [after]), (3, False, [before])]
    tiles += [(o, True, [swap(p) for p in tile]) for o, _, tile in tiles]
    tiles += [(2, False, far), (2, True, [swap(p) for p in far])]
    *grads, mark = weight_grads(coords, tiles, pieces)
    input_grad = sum_shares(shares, mark)
    return (input_grad, *grads)


def solution(mesh):
    fine = Mesh(mesh.devices.reshape(4, 2, 4, 4), ("x", "c", "y", "z"))
    dp, tensor = ("x", "c"), ("y", "z")
    in_specs = (
        P(dp, tensor),
        P(dp, tensor),
        P(None, tensor),
        P(None, tensor),
        P(tensor, None),
        P(dp, None),
        P(dp),
    )
    out_specs = (P(dp, tensor), P(dp, tensor), P(dp, tensor), P(tensor, dp))
    return jax.shard_map(
        per_device, mesh=fine, in_specs=in_specs, out_specs=out_specs, check_vma=False
    )
```

```python
import jax
import jax.numpy as jnp
from jax import lax
from jax.experimental import pallas as pl
from jax.experimental.pallas import tpu as pltpu
from jax.sharding import Mesh, PartitionSpec as P

BLOCK = 128
RING = 4
OFFSETS = (0, 1, 3, 2)
MIB = 2**20

IN_VMEM = pl.BlockSpec(memory_space=pltpu.VMEM)
IN_SMEM = pl.BlockSpec(memory_space=pltpu.SMEM)
ANYWHERE = pl.BlockSpec(memory_space=pl.ANY)


def from_offset(value, axis, offset):
    return lax.ppermute(value, axis, [(i, (i - offset) % RING) for i in range(RING)])


def place_of(offset):
    offset = lax.rem(offset + RING, RING)
    return jnp.where(offset < 2, offset, 5 - offset)


def nn(a, b):
    return jnp.dot(a, b, preferred_element_type=jnp.float32)


def nt(a, b):
    return lax.dot_general(a, b, (((1,), (1,)), ((), ())), preferred_element_type=jnp.float32)


def tn(a, b):
    return lax.dot_general(a, b, (((0,), (0,)), ((), ())), preferred_element_type=jnp.float32)


def relay(value, *behind):
    def kernel(*refs):
        refs[-1][...] = refs[0][...]

    return pl.pallas_call(
        kernel,
        in_specs=[IN_VMEM] + [ANYWHERE] * len(behind),
        out_specs=IN_VMEM,
        out_shape=jax.ShapeDtypeStruct(value.shape, value.dtype),
        compiler_params=pltpu.CompilerParams(vmem_limit_bytes=4 * MIB),
        cost_estimate=pl.CostEstimate(
            flops=0, bytes_accessed=4 * value.size, transcendentals=0
        ),
        name="relay",
    )(value, *behind)


def halves(after, before, behind):
    rows, cols = after.shape
    half = rows // 2

    def kernel(after, before, behind, low, high, sems):
        copies = [
            pltpu.make_async_copy(after.at[pl.ds(0, half)], low, sems.at[0]),
            pltpu.make_async_copy(before.at[pl.ds(half, half)], high, sems.at[1]),
        ]
        for copy in copies:
            copy.start()
        for copy in copies:
            copy.wait()

    return pl.pallas_call(
        kernel,
        in_specs=[ANYWHERE] * 3,
        out_specs=[IN_VMEM] * 2,
        out_shape=[jax.ShapeDtypeStruct((half, cols), after.dtype)] * 2,
        scratch_shapes=[pltpu.SemaphoreType.DMA((2,))],
        compiler_params=pltpu.CompilerParams(vmem_limit_bytes=4 * MIB),
        cost_estimate=pl.CostEstimate(
            flops=0, bytes_accessed=4 * rows * cols, transcendentals=0
        ),
        name="halves",
    )(after, before, behind)


def group_buffers(depth, f_local, count):
    return [
        pltpu.VMEM((count, 4 * depth, f_local), jnp.bfloat16),
        pltpu.VMEM((count, 4 * depth, f_local), jnp.bfloat16),
        pltpu.VMEM((count, f_local, 4 * depth), jnp.bfloat16),
        pltpu.SemaphoreType.DMA((6 * count,)),
    ]


def fetch_group(coords, s, offset, weights, buffers):
    wg, wu, wd = weights
    wg_buf, wu_buf, wd_buf, sems = buffers
    wide = wg_buf.shape[1]
    depth = wide // 4
    row, col = lax.rem(coords[2] + offset, 4), lax.rem(coords[3] + offset, 4)
    rows = pl.ds(pl.multiple_of(row * wide, wide), wide)
    views = [(wg.at[rows], wg_buf.at[s]), (wu.at[rows], wu_buf.at[s])]
    for k in range(4):
        cols = pl.ds(pl.multiple_of((4 * k + col) * depth, depth), depth)
        views.append((wd.at[:, cols], wd_buf.at[s, :, pl.ds(k * depth, depth)]))
    copies = [
        pltpu.make_async_copy(source, target, sems.at[6 * s + j])
        for j, (source, target) in enumerate(views)
    ]
    for copy in copies:
        copy.start()
    return copies


def group_terms(coords, s, x, dy, copies, buffers):
    y, z = coords[2], coords[3]
    x = jnp.concatenate([x[place_of(k - z)] for k in range(4)], axis=1)
    copies[0].wait()
    yield nn(x, buffers[0][s])
    copies[1].wait()
    yield nn(x, buffers[1][s])
    dy = jnp.concatenate([dy[place_of(k - y)] for k in range(4)], axis=1)
    for copy in copies[2:]:
        copy.wait()
    yield nt(dy, buffers[2][s])


def forward_first(coords, x, dy, weights):
    rows, depth = x.shape[1:]
    f_local = weights[0].shape[1]

    def kernel(coords, x, dy, wg, wu, wd, *refs):
        outs, held, sems, buffers = refs[:3], refs[3], refs[4], refs[5:]
        loads = [
            pltpu.make_async_copy(piece, held.at[k], sems.at[k]) for k, piece in enumerate((x, dy))
        ]
        for load in loads:
            load.start()
        copies = fetch_group(coords, 0, 0, (wg, wu, wd), buffers)
        for load in loads:
            load.wait()
        for out, term in zip(outs, group_terms(coords, 0, held.at[0], held.at[1], copies, buffers)):
            out[...] = term

    return pl.pallas_call(
        kernel,
        in_specs=[IN_SMEM] + [ANYWHERE] * 5,
        out_specs=[IN_VMEM] * 3,
        out_shape=[jax.ShapeDtypeStruct((rows, f_local), jnp.float32)] * 3,
        scratch_shapes=[
            pltpu.VMEM((2, 4, rows, depth), jnp.bfloat16),
            pltpu.SemaphoreType.DMA((2,)),
        ]
        + group_buffers(depth, f_local, 1),
        compiler_params=pltpu.CompilerParams(vmem_limit_bytes=48 * MIB),
        cost_estimate=pl.CostEstimate(
            flops=24 * rows * depth * f_local,
            bytes_accessed=24 * depth * f_local,
            transcendentals=0,
        ),
        name="forward_first",
    )(coords, x, dy, *weights)


def forward_more(coords, offsets, xs, dys, weights, sums, active):
    count = len(offsets)
    rows, depth = xs[0].shape[1:]
    f_local = weights[0].shape[1]
    nblk = f_local // BLOCK
    last = active is not None

    def kernel(coords, *refs):
        on, refs = (refs[0], refs[1:]) if last else (None, refs)
        pieces, weights = refs[: 2 * count], refs[2 * count : 2 * count + 3]
        olds, refs = refs[2 * count + 3 : 2 * count + 6], refs[2 * count + 6 :]
        outs, refs = (refs[:1], refs[1:]) if last else (refs[:3], refs[3:])
        accs, old_bufs, held, sems, buffers = refs[:3], refs[3:6], refs[6], refs[7], refs[8:]
        groups = []
        for s, offset in enumerate(offsets):
            loads = [
                pltpu.make_async_copy(pieces[k], held.at[k], sems.at[k]) for k in (s, count + s)
            ]
            for load in loads:
                load.start()
            groups.append((loads, fetch_group(coords, s, offset, weights, buffers)))
        old_loads = [
            pltpu.make_async_copy(old, old_buf, sems.at[2 * count + k])
            for k, (old, old_buf) in enumerate(zip(olds, old_bufs))
        ]
        for load in old_loads:
            load.start()
        for s, (loads, copies) in enumerate(groups):
            for load in loads:
                load.wait()
            terms = group_terms(coords, s, held.at[s], held.at[count + s], copies, buffers)
            for acc, term in zip(accs, terms):
                acc[...] = term if s == 0 else acc[...] + term
        for load in old_loads:
            load.wait()
        if not last:
            for out, acc, old in zip(outs, accs, old_bufs):
                out[...] = acc[...] + old[...]
            return
        for b in range(nblk):
            cols = pl.ds(b * BLOCK, BLOCK)
            gate, up, hid = (acc[:, cols] + old[:, cols] for acc, old in zip(accs, old_bufs))
            logistic = jax.nn.sigmoid(gate)
            swish = gate * logistic
            values = (
                swish * up,
                hid * up * logistic * (1.0 + gate * (1.0 - logistic)),
                hid * swish,
            )
            for k, value in enumerate(values):
                outs[0][:, pl.ds(k * f_local + b * BLOCK, BLOCK)] = jnp.where(
                    on[b] > 0, value, 0.0
                ).astype(outs[0].dtype)

    act_shape = jax.ShapeDtypeStruct((rows, 3 * f_local), jnp.bfloat16)
    sum_shape = jax.ShapeDtypeStruct((rows, f_local), jnp.float32)
    return pl.pallas_call(
        kernel,
        in_specs=[IN_SMEM] * (2 if last else 1) + [ANYWHERE] * (2 * count + 6),
        out_specs=IN_VMEM if last else [IN_VMEM] * 3,
        out_shape=act_shape if last else [sum_shape] * 3,
        scratch_shapes=[pltpu.VMEM((rows, f_local), jnp.float32)] * 6
        + [
            pltpu.VMEM((2 * count, 4, rows, depth), jnp.bfloat16),
            pltpu.SemaphoreType.DMA((2 * count + 3,)),
        ]
        + group_buffers(depth, f_local, count),
        compiler_params=pltpu.CompilerParams(vmem_limit_bytes=48 * MIB),
        cost_estimate=pl.CostEstimate(
            flops=24 * count * rows * depth * f_local,
            bytes_accessed=24 * count * depth * f_local,
            transcendentals=rows * f_local if last else 0,
        ),
        name="forward_last" if last else "forward_near",
    )(coords, *([active] if last else []), *xs, *dys, *weights, *sums)


def backward(act, wg, wu):
    rows = act.shape[0]
    d_model, f_local = wg.shape
    n = 16
    depth = d_model // n
    wide = 4 * depth

    def kernel(act, wg, wu, out, wg_buf, wu_buf, sems):
        copies = []
        for i in range(4):
            at = pl.ds(i * wide, wide)
            copies.append(
                (
                    pltpu.make_async_copy(wg.at[at], wg_buf.at[at], sems.at[2 * i]),
                    pltpu.make_async_copy(wu.at[at], wu_buf.at[at], sems.at[2 * i + 1]),
                )
            )
        for pair in copies:
            for copy in pair:
                copy.start()
        d_gate, d_up = (act[:, pl.ds(k * f_local, f_local)] for k in (1, 2))
        for i, pair in enumerate(copies):
            at = pl.ds(i * wide, wide)
            for copy in pair:
                copy.wait()
            total = (nt(d_gate, wg_buf[at]) + nt(d_up, wu_buf[at])).astype(out.dtype)
            for k in range(4):
                out[4 * i + k] = total[:, k * depth : (k + 1) * depth]

    return pl.pallas_call(
        kernel,
        in_specs=[IN_VMEM] + [ANYWHERE] * 2,
        out_specs=IN_VMEM,
        out_shape=jax.ShapeDtypeStruct((n, rows, depth), jnp.bfloat16),
        scratch_shapes=[
            pltpu.VMEM(wg.shape, jnp.bfloat16),
            pltpu.VMEM(wu.shape, jnp.bfloat16),
            pltpu.SemaphoreType.DMA((8,)),
        ],
        compiler_params=pltpu.CompilerParams(vmem_limit_bytes=50 * MIB),
        cost_estimate=pl.CostEstimate(
            flops=4 * rows * d_model * f_local,
            bytes_accessed=4 * d_model * f_local,
            transcendentals=0,
        ),
        name="backward",
    )(act, wg, wu)


def weight_grads(coords, tiles, pieces):
    count, chunks = len(tiles), (1, 3, 4)
    parts = [part for _, _, tile in tiles for part in tile]
    wide = parts[0].shape[1]
    rows = pieces.shape[1] // 2
    f_local = wide // 3
    depth = pieces.shape[2]
    cols = 2 * depth
    shapes = [(cols, f_local), (cols, f_local), (f_local, cols)]

    def kernel(coords, *refs):
        acts, refs = list(refs[: len(parts)]), refs[len(parts) :]
        pieces, outs, mark, accs, results = refs[0], refs[1:4], refs[4], refs[5:8], refs[8:11]
        act_buf, tok_buf, cot_buf, sems = refs[11:]
        mark[...] = jnp.zeros_like(mark)
        x, c = coords[0], coords[1]
        used = [0]

        def start(source, target):
            copy = pltpu.make_async_copy(source, target, sems.at[used[0]])
            used[0] += 1
            copy.start()
            return copy

        loads = []
        for t, (offset, other, tile) in enumerate(tiles):
            mine, at = [], t * rows
            for part in tile:
                mine.append(start(acts.pop(0), act_buf.at[pl.ds(at, part.shape[0])]))
                at += part.shape[0]
            core = 1 - c if other else c
            for h in range(2):
                piece = lax.rem(x + offset, RING) * RING + core + 2 * h
                for k, buf in enumerate((tok_buf, cot_buf)):
                    target = buf.at[pl.ds(t * rows, rows), pl.ds(h * depth, depth)]
                    mine.append(start(pieces.at[piece, pl.ds(k * rows, rows)], target))
            loads.append(mine)
        stores = []
        for t, chunk in zip((0, 1, 4), chunks):
            for load in sum(loads[t : t + chunk], []):
                load.wait()
            at = pl.ds(t * rows, chunk * rows)
            for k in range(3):
                if k < 2:
                    term = tn(tok_buf[at], act_buf[at, pl.ds((k + 1) * f_local, f_local)])
                else:
                    term = tn(act_buf[at, pl.ds(0, f_local)], cot_buf[at])
                if t > 0:
                    term = accs[k][...] + term
                if t + chunk < count:
                    accs[k][...] = term
                else:
                    results[k][...] = term.astype(results[k].dtype)
                    stores.append(start(results[k], outs[k]))
        for store in stores:
            store.wait()

    return pl.pallas_call(
        kernel,
        in_specs=[IN_SMEM] + [ANYWHERE] * (len(parts) + 1),
        out_specs=[ANYWHERE] * 3 + [IN_VMEM],
        out_shape=[jax.ShapeDtypeStruct(shape, jnp.bfloat16) for shape in shapes + [(16, 128)]],
        scratch_shapes=[pltpu.VMEM(shape, jnp.float32) for shape in shapes]
        + [pltpu.VMEM(shape, jnp.bfloat16) for shape in shapes]
        + [
            pltpu.VMEM((count * rows, wide), jnp.bfloat16),
            pltpu.VMEM((count * rows, cols), jnp.bfloat16),
            pltpu.VMEM((count * rows, cols), jnp.bfloat16),
            pltpu.SemaphoreType.DMA((len(parts) + 4 * count + 3,)),
        ],
        compiler_params=pltpu.CompilerParams(vmem_limit_bytes=58 * MIB),
        cost_estimate=pl.CostEstimate(
            flops=4 * count * rows * depth * wide,
            bytes_accessed=2 * count * rows * (wide + 4 * depth),
            transcendentals=0,
        ),
        name="weight_grads",
    )(coords, *parts, pieces)


def sum_shares(shares, behind):
    n, rows, cols = shares.shape

    def kernel(shares, behind, out):
        total = shares[0].astype(jnp.float32)
        for k in range(1, n):
            total += shares[k].astype(jnp.float32)
        out[...] = total.astype(out.dtype)

    return pl.pallas_call(
        kernel,
        in_specs=[IN_VMEM, ANYWHERE],
        out_specs=IN_VMEM,
        out_shape=jax.ShapeDtypeStruct((rows, cols), shares.dtype),
        compiler_params=pltpu.CompilerParams(vmem_limit_bytes=8 * MIB),
        cost_estimate=pl.CostEstimate(
            flops=n * rows * cols, bytes_accessed=2 * n * rows * cols, transcendentals=0
        ),
        name="sum_shares",
    )(shares, behind)


def to_columns():
    order = [(x, c, y, z) for x in range(4) for c in range(2) for y in range(4) for z in range(4)]
    flat = lambda x, c, y, z: ((x * 2 + c) * 4 + y) * 4 + z
    return [(flat(x, c, y, z), flat(y, z // 2, x, z % 2 * 2 + c)) for x, c, y, z in order]


def per_device(tokens, grad_out, w_gate, w_up, w_down, active_ids, active_count):
    rows, depth = tokens.shape
    half = rows // 2
    f_local = w_gate.shape[1]
    nblk = f_local // BLOCK
    x, c, y, z = (lax.axis_index(a) for a in ("x", "c", "y", "z"))
    coords = jnp.stack([x, c, y, z]).astype(jnp.int32)

    tok, cot = tokens[None], grad_out[None]
    tok_near = [from_offset(tok, "z", o) for o in OFFSETS[1:]]
    cot_near = [from_offset(cot, "y", o) for o in OFFSETS[1:]]
    tok_row = jnp.concatenate([tok] + tok_near, axis=0)
    cot_row = jnp.concatenate([cot] + cot_near, axis=0)
    tok_after, tok_before = from_offset(tok_row, "y", 1), from_offset(tok_row, "y", 3)
    cot_after, cot_before = from_offset(cot_row, "z", 1), from_offset(cot_row, "z", 3)
    tok_low = from_offset(tok_after[:, :half], "y", 1)
    tok_high = from_offset(tok_before[:, half:], "y", 3)
    cot_low = from_offset(cot_after[:, :half], "z", 1)
    cot_high = from_offset(cot_before[:, half:], "z", 3)
    tok_far = jnp.concatenate([tok_low, tok_high], axis=1)
    cot_far = jnp.concatenate([cot_low, cot_high], axis=1)

    block_ids = (y * 4 + z) * nblk + jnp.arange(nblk, dtype=jnp.int32)
    listed = jnp.arange(active_ids.shape[1], dtype=jnp.int32) < active_count[0]
    matches = (active_ids[0][:, None] == block_ids[None, :]) & listed[:, None]
    active = jnp.any(matches, axis=0).astype(jnp.int32)

    weights = (w_gate, w_up, w_down)
    sums = forward_first(coords, tok_row, cot_row, weights)
    sums = forward_more(
        coords, [1, 3], [tok_after, tok_before], [cot_after, cot_before], weights, sums, None
    )
    both = jnp.concatenate([tokens, grad_out], axis=0)
    turned = lax.ppermute(both, ("x", "c", "y", "z"), to_columns())
    pieces = lax.all_gather(relay(turned, tok_far, cot_far, sums[0]), ("y", "z"))

    act = forward_more(coords, [2], [tok_far], [cot_far], weights, sums, active)

    after, before = from_offset(act, "x", 1), from_offset(act, "x", 3)
    partial_dx = backward(act, w_gate, w_up)
    shares = lax.all_to_all(partial_dx, ("y", "z"), 0, 0)
    low, high = halves(after, before, partial_dx)
    far = [from_offset(low, "x", 1), from_offset(high, "x", 3)]
    swap = lambda a: lax.ppermute(a, "c", [(0, 1), (1, 0)])
    tiles = [(0, False, [act]), (1, False, [after]), (3, False, [before])]
    tiles += [(o, True, [swap(p) for p in tile]) for o, _, tile in tiles]
    tiles += [(2, False, far), (2, True, [swap(p) for p in far])]
    *grads, mark = weight_grads(coords, tiles, pieces)
    input_grad = sum_shares(shares, mark)
    return (input_grad, *grads)


def solution(mesh):
    fine = Mesh(mesh.devices.reshape(4, 2, 4, 4), ("x", "c", "y", "z"))
    dp, tensor = ("x", "c"), ("y", "z")
    in_specs = (
        P(dp, tensor),
        P(dp, tensor),
        P(None, tensor),
        P(None, tensor),
        P(tensor, None),
        P(dp, None),
        P(dp),
    )
    out_specs = (P(dp, tensor), P(dp, tensor), P(dp, tensor), P(tensor, dp))
    return jax.shard_map(
        per_device, mesh=fine, in_specs=in_specs, out_specs=out_specs, check_vma=False
    )
```

```python
import jax
import jax.numpy as jnp
from jax import lax
from jax.experimental import pallas as pl
from jax.experimental.pallas import tpu as pltpu
from jax.sharding import Mesh, PartitionSpec as P

BLOCK = 128
RING = 4
OFFSETS = (0, 1, 3, 2)
MIB = 2**20

IN_VMEM = pl.BlockSpec(memory_space=pltpu.VMEM)
IN_SMEM = pl.BlockSpec(memory_space=pltpu.SMEM)
ANYWHERE = pl.BlockSpec(memory_space=pl.ANY)


def from_offset(value, axis, offset):
    return lax.ppermute(value, axis, [(i, (i - offset) % RING) for i in range(RING)])


def place_of(offset):
    offset = lax.rem(offset + RING, RING)
    return jnp.where(offset < 2, offset, 5 - offset)


def nn(a, b):
    return jnp.dot(a, b, preferred_element_type=jnp.float32)


def nt(a, b):
    return lax.dot_general(a, b, (((1,), (1,)), ((), ())), preferred_element_type=jnp.float32)


def tn(a, b):
    return lax.dot_general(a, b, (((0,), (0,)), ((), ())), preferred_element_type=jnp.float32)


def relay(value, *behind):
    def kernel(*refs):
        refs[-1][...] = refs[0][...]

    return pl.pallas_call(
        kernel,
        in_specs=[IN_VMEM] + [ANYWHERE] * len(behind),
        out_specs=IN_VMEM,
        out_shape=jax.ShapeDtypeStruct(value.shape, value.dtype),
        compiler_params=pltpu.CompilerParams(vmem_limit_bytes=4 * MIB),
        cost_estimate=pl.CostEstimate(
            flops=0, bytes_accessed=4 * value.size, transcendentals=0
        ),
        name="relay",
    )(value, *behind)


def halves(after, before, behind):
    rows, cols = after.shape
    half = rows // 2

    def kernel(after, before, behind, low, high, sems):
        copies = [
            pltpu.make_async_copy(after.at[pl.ds(0, half)], low, sems.at[0]),
            pltpu.make_async_copy(before.at[pl.ds(half, half)], high, sems.at[1]),
        ]
        for copy in copies:
            copy.start()
        for copy in copies:
            copy.wait()

    return pl.pallas_call(
        kernel,
        in_specs=[ANYWHERE] * 3,
        out_specs=[IN_VMEM] * 2,
        out_shape=[jax.ShapeDtypeStruct((half, cols), after.dtype)] * 2,
        scratch_shapes=[pltpu.SemaphoreType.DMA((2,))],
        compiler_params=pltpu.CompilerParams(vmem_limit_bytes=4 * MIB),
        cost_estimate=pl.CostEstimate(
            flops=0, bytes_accessed=4 * rows * cols, transcendentals=0
        ),
        name="halves",
    )(after, before, behind)


def group_buffers(depth, f_local, count):
    return [
        pltpu.VMEM((count, 4 * depth, f_local), jnp.bfloat16),
        pltpu.VMEM((count, 4 * depth, f_local), jnp.bfloat16),
        pltpu.VMEM((count, f_local, 4 * depth), jnp.bfloat16),
        pltpu.SemaphoreType.DMA((6 * count,)),
    ]


def fetch_group(coords, s, offset, weights, buffers):
    wg, wu, wd = weights
    wg_buf, wu_buf, wd_buf, sems = buffers
    wide = wg_buf.shape[1]
    depth = wide // 4
    row, col = lax.rem(coords[2] + offset, 4), lax.rem(coords[3] + offset, 4)
    rows = pl.ds(pl.multiple_of(row * wide, wide), wide)
    views = [(wg.at[rows], wg_buf.at[s]), (wu.at[rows], wu_buf.at[s])]
    for k in range(4):
        cols = pl.ds(pl.multiple_of((4 * k + col) * depth, depth), depth)
        views.append((wd.at[:, cols], wd_buf.at[s, :, pl.ds(k * depth, depth)]))
    copies = [
        pltpu.make_async_copy(source, target, sems.at[6 * s + j])
        for j, (source, target) in enumerate(views)
    ]
    for copy in copies:
        copy.start()
    return copies


def group_terms(coords, s, x, dy, copies, buffers):
    y, z = coords[2], coords[3]
    x = jnp.concatenate([x[place_of(k - z)] for k in range(4)], axis=1)
    copies[0].wait()
    yield nn(x, buffers[0][s])
    copies[1].wait()
    yield nn(x, buffers[1][s])
    dy = jnp.concatenate([dy[place_of(k - y)] for k in range(4)], axis=1)
    for copy in copies[2:]:
        copy.wait()
    yield nt(dy, buffers[2][s])


def forward_first(coords, x, dy, weights):
    rows, depth = x.shape[1:]
    f_local = weights[0].shape[1]

    def kernel(coords, x, dy, wg, wu, wd, *refs):
        outs, held, sems, buffers = refs[:3], refs[3], refs[4], refs[5:]
        loads = [
            pltpu.make_async_copy(piece, held.at[k], sems.at[k]) for k, piece in enumerate((x, dy))
        ]
        for load in loads:
            load.start()
        copies = fetch_group(coords, 0, 0, (wg, wu, wd), buffers)
        for load in loads:
            load.wait()
        for out, term in zip(outs, group_terms(coords, 0, held.at[0], held.at[1], copies, buffers)):
            out[...] = term

    return pl.pallas_call(
        kernel,
        in_specs=[IN_SMEM] + [ANYWHERE] * 5,
        out_specs=[IN_VMEM] * 3,
        out_shape=[jax.ShapeDtypeStruct((rows, f_local), jnp.float32)] * 3,
        scratch_shapes=[
            pltpu.VMEM((2, 4, rows, depth), jnp.bfloat16),
            pltpu.SemaphoreType.DMA((2,)),
        ]
        + group_buffers(depth, f_local, 1),
        compiler_params=pltpu.CompilerParams(vmem_limit_bytes=50 * MIB),
        cost_estimate=pl.CostEstimate(
            flops=24 * rows * depth * f_local,
            bytes_accessed=24 * depth * f_local,
            transcendentals=0,
        ),
        name="forward_first",
    )(coords, x, dy, *weights)


def forward_more(coords, offsets, xs, dys, weights, sums, active):
    count = len(offsets)
    rows, depth = xs[0].shape[1:]
    f_local = weights[0].shape[1]
    nblk = f_local // BLOCK
    last = active is not None

    def kernel(coords, *refs):
        on, refs = (refs[0], refs[1:]) if last else (None, refs)
        pieces, weights = refs[: 2 * count], refs[2 * count : 2 * count + 3]
        olds, refs = refs[2 * count + 3 : 2 * count + 6], refs[2 * count + 6 :]
        outs, refs = (refs[:1], refs[1:]) if last else (refs[:3], refs[3:])
        accs, old_bufs, held, sems, buffers = refs[:3], refs[3:6], refs[6], refs[7], refs[8:]
        groups = []
        for s, offset in enumerate(offsets):
            loads = [
                pltpu.make_async_copy(pieces[k], held.at[k], sems.at[k]) for k in (s, count + s)
            ]
            for load in loads:
                load.start()
            groups.append((loads, fetch_group(coords, s, offset, weights, buffers)))
        old_loads = [
            pltpu.make_async_copy(old, old_buf, sems.at[2 * count + k])
            for k, (old, old_buf) in enumerate(zip(olds, old_bufs))
        ]
        for load in old_loads:
            load.start()
        for s, (loads, copies) in enumerate(groups):
            for load in loads:
                load.wait()
            terms = group_terms(coords, s, held.at[s], held.at[count + s], copies, buffers)
            for acc, term in zip(accs, terms):
                acc[...] = term if s == 0 else acc[...] + term
        for load in old_loads:
            load.wait()
        if not last:
            for out, acc, old in zip(outs, accs, old_bufs):
                out[...] = acc[...] + old[...]
            return
        for b in range(nblk):
            cols = pl.ds(b * BLOCK, BLOCK)
            gate, up, hid = (acc[:, cols] + old[:, cols] for acc, old in zip(accs, old_bufs))
            logistic = jax.nn.sigmoid(gate)
            swish = gate * logistic
            values = (
                swish * up,
                hid * up * logistic * (1.0 + gate * (1.0 - logistic)),
                hid * swish,
            )
            for k, value in enumerate(values):
                outs[0][:, pl.ds(k * f_local + b * BLOCK, BLOCK)] = jnp.where(
                    on[b] > 0, value, 0.0
                ).astype(outs[0].dtype)

    act_shape = jax.ShapeDtypeStruct((rows, 3 * f_local), jnp.bfloat16)
    sum_shape = jax.ShapeDtypeStruct((rows, f_local), jnp.float32)
    return pl.pallas_call(
        kernel,
        in_specs=[IN_SMEM] * (2 if last else 1) + [ANYWHERE] * (2 * count + 6),
        out_specs=IN_VMEM if last else [IN_VMEM] * 3,
        out_shape=act_shape if last else [sum_shape] * 3,
        scratch_shapes=[pltpu.VMEM((rows, f_local), jnp.float32)] * 6
        + [
            pltpu.VMEM((2 * count, 4, rows, depth), jnp.bfloat16),
            pltpu.SemaphoreType.DMA((2 * count + 3,)),
        ]
        + group_buffers(depth, f_local, count),
        compiler_params=pltpu.CompilerParams(vmem_limit_bytes=50 * MIB),
        cost_estimate=pl.CostEstimate(
            flops=24 * count * rows * depth * f_local,
            bytes_accessed=24 * count * depth * f_local,
            transcendentals=rows * f_local if last else 0,
        ),
        name="forward_last" if last else "forward_near",
    )(coords, *([active] if last else []), *xs, *dys, *weights, *sums)


def backward(act, wg, wu):
    rows = act.shape[0]
    d_model, f_local = wg.shape
    n = 16
    depth = d_model // n
    wide = 4 * depth

    def kernel(act, wg, wu, out, wg_buf, wu_buf, sems):
        copies = []
        for i in range(4):
            at = pl.ds(i * wide, wide)
            copies.append(
                (
                    pltpu.make_async_copy(wg.at[at], wg_buf.at[at], sems.at[2 * i]),
                    pltpu.make_async_copy(wu.at[at], wu_buf.at[at], sems.at[2 * i + 1]),
                )
            )
        for pair in copies:
            for copy in pair:
                copy.start()
        d_gate, d_up = (act[:, pl.ds(k * f_local, f_local)] for k in (1, 2))
        for i, pair in enumerate(copies):
            at = pl.ds(i * wide, wide)
            for copy in pair:
                copy.wait()
            total = (nt(d_gate, wg_buf[at]) + nt(d_up, wu_buf[at])).astype(out.dtype)
            for k in range(4):
                out[4 * i + k] = total[:, k * depth : (k + 1) * depth]

    return pl.pallas_call(
        kernel,
        in_specs=[IN_VMEM] + [ANYWHERE] * 2,
        out_specs=IN_VMEM,
        out_shape=jax.ShapeDtypeStruct((n, rows, depth), jnp.bfloat16),
        scratch_shapes=[
            pltpu.VMEM(wg.shape, jnp.bfloat16),
            pltpu.VMEM(wu.shape, jnp.bfloat16),
            pltpu.SemaphoreType.DMA((8,)),
        ],
        compiler_params=pltpu.CompilerParams(vmem_limit_bytes=50 * MIB),
        cost_estimate=pl.CostEstimate(
            flops=4 * rows * d_model * f_local,
            bytes_accessed=4 * d_model * f_local,
            transcendentals=0,
        ),
        name="backward",
    )(act, wg, wu)


def weight_grads(coords, tiles, pieces, shares):
    count, chunks = len(tiles), (1, 3, 4)
    parts = [part for _, _, tile in tiles for part in tile]
    wide = parts[0].shape[1]
    rows = pieces.shape[1] // 2
    f_local = wide // 3
    depth = pieces.shape[2]
    cols = 2 * depth
    shapes = [(cols, f_local), (cols, f_local), (f_local, cols)]

    def kernel(coords, *refs):
        acts, refs = list(refs[: len(parts)]), refs[len(parts) :]
        pieces, shares, outs, accs, results = refs[0], refs[1], refs[2:6], refs[6:9], refs[9:13]
        share_buf, act_buf, tok_buf, cot_buf, sems = refs[13:]
        x, c = coords[0], coords[1]
        used = [0]

        def start(source, target):
            copy = pltpu.make_async_copy(source, target, sems.at[used[0]])
            used[0] += 1
            copy.start()
            return copy

        loads = []
        for t, (offset, other, tile) in enumerate(tiles):
            mine, at = [], t * rows
            for part in tile:
                mine.append(start(acts.pop(0), act_buf.at[pl.ds(at, part.shape[0])]))
                at += part.shape[0]
            core = 1 - c if other else c
            for h in range(2):
                piece = lax.rem(x + offset, RING) * RING + core + 2 * h
                for k, buf in enumerate((tok_buf, cot_buf)):
                    target = buf.at[pl.ds(t * rows, rows), pl.ds(h * depth, depth)]
                    mine.append(start(pieces.at[piece, pl.ds(k * rows, rows)], target))
            loads.append(mine)
        share_load = start(shares, share_buf)
        stores = []
        for t, chunk in zip((0, 1, 4), chunks):
            for load in sum(loads[t : t + chunk], []):
                load.wait()
            at = pl.ds(t * rows, chunk * rows)
            for k in range(3):
                if k < 2:
                    term = tn(tok_buf[at], act_buf[at, pl.ds((k + 1) * f_local, f_local)])
                else:
                    term = tn(act_buf[at, pl.ds(0, f_local)], cot_buf[at])
                if t > 0:
                    term = accs[k][...] + term
                if t + chunk < count:
                    accs[k][...] = term
                else:
                    results[k][...] = term.astype(results[k].dtype)
                    stores.append(start(results[k], outs[k]))
        share_load.wait()
        total = share_buf[0].astype(jnp.float32)
        for k in range(1, shares.shape[0]):
            total += share_buf[k].astype(jnp.float32)
        results[3][...] = total.astype(results[3].dtype)
        stores.append(start(results[3], outs[3]))
        for store in stores:
            store.wait()

    out_shapes = shapes + [shares.shape[1:]]
    return pl.pallas_call(
        kernel,
        in_specs=[IN_SMEM] + [ANYWHERE] * (len(parts) + 2),
        out_specs=[ANYWHERE] * 4,
        out_shape=[jax.ShapeDtypeStruct(shape, jnp.bfloat16) for shape in out_shapes],
        scratch_shapes=[pltpu.VMEM(shape, jnp.float32) for shape in shapes]
        + [pltpu.VMEM(shape, jnp.bfloat16) for shape in out_shapes + [shares.shape]]
        + [
            pltpu.VMEM((count * rows, wide), jnp.bfloat16),
            pltpu.VMEM((count * rows, cols), jnp.bfloat16),
            pltpu.VMEM((count * rows, cols), jnp.bfloat16),
            pltpu.SemaphoreType.DMA((len(parts) + 4 * count + 5,)),
        ],
        compiler_params=pltpu.CompilerParams(vmem_limit_bytes=58 * MIB),
        cost_estimate=pl.CostEstimate(
            flops=4 * count * rows * depth * wide,
            bytes_accessed=2 * count * rows * (wide + 4 * depth),
            transcendentals=0,
        ),
        name="weight_grads",
    )(coords, *parts, pieces, shares)


def to_columns():
    order = [(x, c, y, z) for x in range(4) for c in range(2) for y in range(4) for z in range(4)]
    flat = lambda x, c, y, z: ((x * 2 + c) * 4 + y) * 4 + z
    return [(flat(x, c, y, z), flat(y, z // 2, x, z % 2 * 2 + c)) for x, c, y, z in order]


def per_device(tokens, grad_out, w_gate, w_up, w_down, active_ids, active_count):
    rows, depth = tokens.shape
    half = rows // 2
    f_local = w_gate.shape[1]
    nblk = f_local // BLOCK
    x, c, y, z = (lax.axis_index(a) for a in ("x", "c", "y", "z"))
    coords = jnp.stack([x, c, y, z]).astype(jnp.int32)

    tok, cot = tokens[None], grad_out[None]
    tok_near = [from_offset(tok, "z", o) for o in OFFSETS[1:]]
    cot_near = [from_offset(cot, "y", o) for o in OFFSETS[1:]]
    tok_row = jnp.concatenate([tok] + tok_near, axis=0)
    cot_row = jnp.concatenate([cot] + cot_near, axis=0)
    tok_after, tok_before = from_offset(tok_row, "y", 1), from_offset(tok_row, "y", 3)
    cot_after, cot_before = from_offset(cot_row, "z", 1), from_offset(cot_row, "z", 3)
    tok_low = from_offset(tok_after[:, :half], "y", 1)
    tok_high = from_offset(tok_before[:, half:], "y", 3)
    cot_low = from_offset(cot_after[:, :half], "z", 1)
    cot_high = from_offset(cot_before[:, half:], "z", 3)
    tok_far = jnp.concatenate([tok_low, tok_high], axis=1)
    cot_far = jnp.concatenate([cot_low, cot_high], axis=1)

    block_ids = (y * 4 + z) * nblk + jnp.arange(nblk, dtype=jnp.int32)
    listed = jnp.arange(active_ids.shape[1], dtype=jnp.int32) < active_count[0]
    matches = (active_ids[0][:, None] == block_ids[None, :]) & listed[:, None]
    active = jnp.any(matches, axis=0).astype(jnp.int32)

    weights = (w_gate, w_up, w_down)
    sums = forward_first(coords, tok_row, cot_row, weights)
    sums = forward_more(
        coords, [1, 3], [tok_after, tok_before], [cot_after, cot_before], weights, sums, None
    )
    both = jnp.concatenate([tokens, grad_out], axis=0)
    turned = lax.ppermute(both, ("x", "c", "y", "z"), to_columns())
    pieces = lax.all_gather(relay(turned, tok_far, cot_far, sums[0]), ("y", "z"))

    act = forward_more(coords, [2], [tok_far], [cot_far], weights, sums, active)

    after, before = from_offset(act, "x", 1), from_offset(act, "x", 3)
    partial_dx = backward(act, w_gate, w_up)
    shares = lax.all_to_all(partial_dx, ("y", "z"), 0, 0)
    low, high = halves(after, before, partial_dx)
    far = [from_offset(low, "x", 1), from_offset(high, "x", 3)]
    swap = lambda a: lax.ppermute(a, "c", [(0, 1), (1, 0)])
    tiles = [(0, False, [act]), (1, False, [after]), (3, False, [before])]
    tiles += [(o, True, [swap(p) for p in tile]) for o, _, tile in tiles]
    tiles += [(2, False, far), (2, True, [swap(p) for p in far])]
    *grads, input_grad = weight_grads(coords, tiles, pieces, shares)
    return (input_grad, *grads)


def solution(mesh):
    fine = Mesh(mesh.devices.reshape(4, 2, 4, 4), ("x", "c", "y", "z"))
    dp, tensor = ("x", "c"), ("y", "z")
    in_specs = (
        P(dp, tensor),
        P(dp, tensor),
        P(None, tensor),
        P(None, tensor),
        P(tensor, None),
        P(dp, None),
        P(dp),
    )
    out_specs = (P(dp, tensor), P(dp, tensor), P(dp, tensor), P(tensor, dp))
    return jax.shard_map(
        per_device, mesh=fine, in_specs=in_specs, out_specs=out_specs, check_vma=False
    )
```
